32 devices in a mesh: grp: 4 (over z), dev: 8 (over y, x, core).
Axes of the slice: x: 2, y: 2, z: 4, core: 2. Of those that a mesh axis runs over, the one named last changes fastest.
Arguments:
- features: bfloat16 [512, 4800, 128], P(('grp', 'dev'))
- inv_depth: float32 [512, 4800], P(('grp', 'dev')), may hold values from 0.2 to 1
- positions: float32 [3, 512], replicated, may hold values from -0.1 to 0.1
- edge_list: int32 [128, 2], P(('grp', 'dev')), may hold values from -1 to 511, as said below
- edge_counts: int32 [32], P(('grp', 'dev')), may hold values from 2 to 4, as said below
Outputs:
- schur_band: float32 [5, 36, 512], P(None, None, ('grp', 'dev'))
- schur_rhs: float32 [6, 512], P(None, ('grp', 'dev'))
The draws below stay inside these ranges and needn't reach their ends.
Inputs may be any that keep to these rules, and one draw needn't show every extreme that they name: Device d (index grp * 8 + dev) uses its slots d * 4 to d * 4 + edge_counts[d] - 1; some device uses all 4. `edge_list`: in a used slot of device d the source frame lies in d * 16 to d * 16 + 15 and the target differs from it by 1 to 2 frames; unused slots hold -1 in both columns.
All inputs are finite; a program needn't handle non-finite values.
Results may differ from the reference program's by a relative error of at most 0.00034.
Values may be sent and summed in bfloat16 or wider, within the bound.
A program may use at most 128 MiB of HBM per device.

```python
import math
import jax
import jax.numpy as jnp
from jax import lax

C = 128
IMG_H = 60
IMG_W = 80
F_DEV = 16
SPAN = 2
CAP = 4
PIX = 4800
FRAMES = 512
SLOTS = 128


def draw_features(key, part):
    rough_seed = jax.random.normal(jax.random.fold_in(key, 1), (IMG_H, IMG_W, C), jnp.float32)
    rough = rough_seed + jnp.roll(rough_seed, -1, axis=1)
    rough = rough + jnp.roll(rough, -1, axis=0)
    rough = (0.5 * rough).reshape(PIX, C)
    pixel_ids = jnp.arange(PIX, dtype=jnp.int32)
    pixel_row = pixel_ids // IMG_W
    pixel_col = pixel_ids % IMG_W
    row_float = pixel_row.astype(jnp.float32)
    col_float = pixel_col.astype(jnp.float32)
    freq_x = jax.random.randint(jax.random.fold_in(key, 2), (4,), 1, 3).astype(jnp.float32)
    freq_y = jax.random.randint(jax.random.fold_in(key, 3), (4,), 0, 3).astype(jnp.float32)
    phases = jax.random.uniform(jax.random.fold_in(key, 4), (4,), jnp.float32, 0.0, 2.0 * math.pi)
    mode_weights = jax.random.normal(jax.random.fold_in(key, 5), (4, C), jnp.float32)
    smooth = jnp.zeros((PIX, C), jnp.float32)
    for mode in range(4):
        angle = 2.0 * math.pi * (freq_x[mode] * col_float / IMG_W + freq_y[mode] * row_float / IMG_H) + phases[mode]
        smooth = smooth + jnp.cos(angle)[:, None] * mode_weights[mode][None, :]
    smooth = 0.7071 * smooth
    texture = 0.75 * rough + 0.35 * smooth
    shift_row = jax.random.randint(jax.random.fold_in(key, 6), (FRAMES, 1), 0, IMG_H)
    shift_col = jax.random.randint(jax.random.fold_in(key, 7), (FRAMES, 1), 0, IMG_W)
    zoom = jax.random.randint(jax.random.fold_in(key, 8), (FRAMES, 1), -2, 3)
    tex_row = (pixel_row[None, :] + shift_row + (pixel_row[None, :] - IMG_H // 2) * zoom // 8) % IMG_H
    tex_col = (pixel_col[None, :] + shift_col + (pixel_col[None, :] - IMG_W // 2) * zoom // 8) % IMG_W
    warped = tex_row * IMG_W + tex_col
    occluded = jax.random.randint(jax.random.fold_in(key, 9), (FRAMES, PIX), 0, 8) == 0
    random_index = jax.random.randint(jax.random.fold_in(key, 10), (FRAMES, PIX), 0, PIX)
    tex_index = jnp.where(occluded, random_index, warped).astype(jnp.int32)
    moved = texture[tex_index]
    noise_part = 0.5 * jax.random.normal(jax.random.fold_in(key, 11), (FRAMES, PIX, C), jnp.float32)
    result = moved + noise_part
    return result.astype(jnp.bfloat16)


def edge_plan(key):
    base_key = jax.random.fold_in(key, 77)
    devices_all = SLOTS // CAP
    draw_level = jax.random.randint(jax.random.fold_in(base_key, 1), (devices_all,), 0, 8)
    counts_drawn = 2 + (draw_level >= 5).astype(jnp.int32) + (draw_level >= 7).astype(jnp.int32)
    busiest = jax.random.randint(jax.random.fold_in(base_key, 2), (), 0, devices_all)
    device_ids = jnp.arange(devices_all, dtype=jnp.int32)
    counts_drawn = jnp.where(device_ids == busiest, CAP, counts_drawn)
    counts_drawn = jnp.where(device_ids == (busiest + 1) % devices_all, 2, counts_drawn)
    counts_drawn = jnp.minimum(counts_drawn, CAP).astype(jnp.int32)
    slot_ids = jnp.arange(SLOTS, dtype=jnp.int32)
    owner_dev = slot_ids // CAP
    slot_place = slot_ids % CAP
    frame_pick = jax.random.randint(jax.random.fold_in(base_key, 3), (SLOTS,), 0, F_DEV)
    frame_pick = jnp.where(slot_place == 0, 0, jnp.where(slot_place == 1, F_DEV - 1, frame_pick))
    source = owner_dev * F_DEV + frame_pick
    offset_draw = jax.random.randint(jax.random.fold_in(base_key, 4), (SLOTS,), 0, 2 * SPAN)
    offset_value = offset_draw - SPAN + (offset_draw >= SPAN).astype(jnp.int32)
    magnitude = jnp.abs(offset_value)
    offset_value = jnp.where(slot_place == 0, -magnitude, jnp.where(slot_place == 1, magnitude, offset_value))
    target = source + offset_value
    target = jnp.where((target < 0) | (target >= FRAMES), source - offset_value, target)
    last_slot = SLOTS - CAP
    source = jnp.where(slot_ids == last_slot, FRAMES - 1, source)
    target = jnp.where(slot_ids == last_slot, FRAMES - 1 - magnitude, target)
    live_slot = slot_place < counts_drawn[owner_dev]
    edge_rows = jnp.where(live_slot[:, None], jnp.stack([source, target], 1), -1).astype(jnp.int32)
    return (counts_drawn, edge_rows)


def draw_edge_counts(key, part):
    return edge_plan(key)[0]


def draw_edge_list(key, part):
    return edge_plan(key)[1]


def shard_levels(key, dims, cuts, least, top_value):
    factor_of = 1.0
    for dim, parts in cuts:
        draws = jax.random.uniform(jax.random.fold_in(jax.random.fold_in(key, 6), dim), (parts,), jnp.float32, least / len(cuts), top_value / len(cuts))
        factor_of = factor_of * jnp.repeat(jnp.exp(draws), dims[dim] // parts).reshape((-1,) + (1,) * (len(dims) - 1 - dim))
    return factor_of


def setup_inputs(seed: int = 0) -> dict:
    key_of = jax.random.split(jax.random.key(seed), 6)
    return {
        "features": draw_features(jax.random.fold_in(key_of[5], 71), 0),
        "inv_depth": jnp.clip(jnp.exp(math.log(1.0) - 1.609438 * jax.random.uniform(key_of[1], (FRAMES, PIX), jnp.float32) ** shard_levels(key_of[1], (FRAMES, PIX), ((0, 32),), -0.2, 0.2)), 0.2, 1.0),
        "positions": jnp.clip(jax.random.uniform(key_of[2], (3, FRAMES), jnp.float32, -0.1, 0.1), -0.1, 0.1),
        "edge_list": draw_edge_list(jax.random.fold_in(key_of[5], 71), 0),
        "edge_counts": draw_edge_counts(jax.random.fold_in(key_of[5], 71), 0),
    }


DAMPING = 0.02
FLOOR = 0.001
HIGHEST_PREC = lax.Precision.HIGHEST

def pixel_grid(img_height, img_width):
    pixel_index = jnp.arange(img_height * img_width, dtype=jnp.int32)
    row_index = (pixel_index // img_width).astype(jnp.float32)
    col_index = (pixel_index % img_width).astype(jnp.float32)
    horizontal = ((col_index + 0.5) / img_width - 0.5) * 1.2
    vertical = ((row_index + 0.5) / img_height - 0.5) * 0.9
    return (horizontal, vertical)

def match_frames(source, target, coord_table):
    pixels, channels = source.shape
    blocks = source.reshape(8, pixels // 8, channels)
    score_scale = 1.0 / math.sqrt(channels)

    def one_block(row_block):
        scores = lax.dot_general(row_block, target, (((1,), (1,)), ((), ())), preferred_element_type=jnp.float32) * score_scale
        squared = scores * scores
        weights = (squared * squared * squared).astype(jnp.bfloat16)
        return lax.dot_general(coord_table, weights, (((1,), (1,)), ((), ())), preferred_element_type=jnp.float32)
    weight_sums = lax.map(one_block, blocks)
    weight_sums = jnp.transpose(weight_sums, (1, 0, 2)).reshape(3, pixels)
    return weight_sums[0:2] / (weight_sums[2:3] + FLOOR)

def linearize(matched, depth_rows, motion, horizontal, vertical, slot_valid):
    motion_x = motion[:, 0:1]
    motion_y = motion[:, 1:2]
    motion_z = motion[:, 2:3]
    denominator = 1.0 + depth_rows * motion_z
    proj_x = (horizontal + depth_rows * motion_x) / denominator
    proj_y = (vertical + depth_rows * motion_y) / denominator
    slot_mask = slot_valid[:, None]
    res_x = (matched[:, 0] - proj_x) * slot_mask
    res_y = (matched[:, 1] - proj_y) * slot_mask
    depth_x = (motion_x - proj_x * motion_z) / denominator * slot_mask
    depth_y = (motion_y - proj_y * motion_z) / denominator * slot_mask
    scaled = depth_rows / denominator
    zero_block = jnp.zeros_like(scaled)
    row_x = jnp.stack([scaled, zero_block, -scaled * proj_x, -proj_x * proj_y, 1.0 + proj_x * proj_x, -proj_y], 1)
    row_y = jnp.stack([zero_block, scaled, -scaled * proj_y, -(1.0 + proj_y * proj_y), proj_x * proj_y, proj_x], 1)
    jacobian = jnp.stack([row_x, row_y], 1) * slot_valid[:, None, None, None]
    residual = jnp.stack([res_x, res_y], 1)
    depth_jac = jnp.stack([depth_x, depth_y], 1)
    return (residual, depth_jac, jacobian)

def slot_terms(residual, depth_jac, jacobian):
    coupling = jacobian[:, 0] * depth_jac[:, 0:1] + jacobian[:, 1] * depth_jac[:, 1:2]
    normal = jnp.einsum('scip,scjp->sij', jacobian, jacobian, precision=HIGHEST_PREC)
    grad_rows = jnp.einsum('scip,scp->si', jacobian, residual, precision=HIGHEST_PREC)
    depth_h = lax.optimization_barrier(jnp.sum(depth_jac * depth_jac, 1))
    depth_b = lax.optimization_barrier(jnp.sum(depth_jac * residual, 1))
    return (coupling, normal, grad_rows, depth_h, depth_b)

def frame_system(depth_hess, depth_grad, coupling, blockdiag, gradsum, span_frames):
    frames, offsets_count, width_six, pixels = coupling.shape
    coupling = coupling.at[:, span_frames].set(-lax.optimization_barrier(jnp.sum(coupling, 1)))
    flat_coupling = coupling.reshape(frames, offsets_count * 6, pixels)
    schur = jnp.einsum('fap,fbp->fab', flat_coupling / depth_hess[:, None, :], flat_coupling, precision=HIGHEST_PREC)
    pulled = jnp.einsum('fap,fp->fa', flat_coupling, depth_grad / depth_hess, precision=HIGHEST_PREC)
    center = lax.optimization_barrier(jnp.sum(blockdiag, 1))
    zero_block = jnp.zeros_like(center)
    row_list = []
    for first_off in range(offsets_count):
        pieces = []
        for second_off in range(offsets_count):
            if first_off == span_frames and second_off == span_frames:
                pieces.append(center)
            elif first_off == second_off:
                pieces.append(blockdiag[:, first_off])
            elif first_off == span_frames:
                pieces.append(-blockdiag[:, second_off])
            elif second_off == span_frames:
                pieces.append(-blockdiag[:, first_off])
            else:
                pieces.append(zero_block)
        row_list.append(jnp.concatenate(pieces, 2))
    hessian = jnp.concatenate(row_list, 1)
    grad_vector = gradsum.at[:, span_frames].set(-lax.optimization_barrier(jnp.sum(gradsum, 1))).reshape(frames, offsets_count * 6)
    system = (hessian - schur) / pixels
    right_side = (grad_vector - pulled) / pixels
    return (system, right_side)

def assemble(system, right_side, span_frames):
    frames = system.shape[0]
    offsets_count = 2 * span_frames + 1
    band_sum = jnp.zeros((offsets_count, 36, frames + 2 * span_frames), jnp.float32)
    rhs_window = jnp.zeros((6, frames + 2 * span_frames), jnp.float32)
    for first_off in range(offsets_count):
        rhs_window = rhs_window.at[:, first_off:first_off + frames].add(right_side[:, 6 * first_off:6 * first_off + 6].T)
        for second_off in range(first_off, offsets_count):
            piece = system[:, 6 * first_off:6 * first_off + 6, 6 * second_off:6 * second_off + 6].reshape(frames, 36)
            band_sum = band_sum.at[second_off - first_off, :, first_off:first_off + frames].add(piece.T)
    return (band_sum, rhs_window)

def reference(features, inv_depth, positions, edge_list, edge_counts):
    frames, pixels, channels = features.shape
    slot_count = edge_list.shape[0]
    offsets_count = 2 * SPAN + 1
    horizontal, vertical = pixel_grid(IMG_H, IMG_W)
    coord_table = jnp.stack([horizontal, vertical, jnp.ones_like(horizontal)]).astype(jnp.bfloat16)
    slot_ids = jnp.arange(slot_count, dtype=jnp.int32)
    valid_flag = (slot_ids % CAP < edge_counts[slot_ids // CAP]) & (edge_list[:, 0] >= 0)
    slot_valid = valid_flag.astype(jnp.float32)
    source = jnp.clip(edge_list[:, 0], 0, frames - 1).astype(jnp.int32)
    target = jnp.clip(edge_list[:, 1], 0, frames - 1).astype(jnp.int32)

    def one_slot(slot_index):
        return lax.cond(valid_flag[slot_index], lambda: match_frames(features[source[slot_index]], features[target[slot_index]], coord_table), lambda: jnp.zeros((2, pixels), jnp.float32))
    matched = lax.map(one_slot, slot_ids)
    motion = (positions[:, target] - positions[:, source]).T
    depth_rows = inv_depth[source]
    residual, depth_jac, jacobian = linearize(matched, depth_rows, motion, horizontal, vertical, slot_valid)
    coupling, normal, grad_rows, depth_h, depth_b = slot_terms(residual, depth_jac, jacobian)
    depth_hess = DAMPING + jax.ops.segment_sum(depth_h, source, frames)
    depth_grad = jax.ops.segment_sum(depth_b, source, frames)
    pair_code = jnp.clip(source * offsets_count + (target - source + SPAN), 0, frames * offsets_count - 1).astype(jnp.int32)
    coupled = jax.ops.segment_sum(coupling.reshape(slot_count, 6 * pixels), pair_code, frames * offsets_count)
    coupled = coupled.reshape(frames, offsets_count, 6, pixels)
    blockdiag = jax.ops.segment_sum(normal.reshape(slot_count, 36), pair_code, frames * offsets_count).reshape(frames, offsets_count, 6, 6)
    gradsum = jax.ops.segment_sum(grad_rows, pair_code, frames * offsets_count).reshape(frames, offsets_count, 6)
    system, right_side = frame_system(depth_hess, depth_grad, coupled, blockdiag, gradsum, SPAN)
    band_sum, rhs_window = assemble(system, right_side, SPAN)
    return (band_sum[:, :, SPAN:SPAN + frames], rhs_window[:, SPAN:SPAN + frames])
```

```python
import functools

import jax
import jax.numpy as jnp
import numpy as np
from jax import lax
from jax.experimental import pallas as pl
from jax.experimental.pallas import tpu as pltpu
from jax.sharding import PartitionSpec as P

IMG_H = 60
IMG_W = 80
SPAN = 2
DAMPING = 0.02
FLOOR = 0.001
HIGHEST_PREC = lax.Precision.HIGHEST
AXES = ("grp", "dev")
ROWS = 8
P_TILES = 2
OFFSETS = 2 * SPAN + 1


def from_behind(value, steps):
    count = lax.axis_size(AXES)
    first, last = (max(0, -steps), min(count, count - steps))
    return lax.ppermute(value, AXES, [(source, source + steps) for source in range(first, last)])


def pixel_grid():
    index = np.arange(IMG_H * IMG_W)
    row = (index // IMG_W).astype(np.float32)
    col = (index % IMG_W).astype(np.float32)
    half = np.float32(0.5)
    horizontal = ((col + half) / np.float32(IMG_W) - half) * np.float32(1.2)
    vertical = ((row + half) / np.float32(IMG_H) - half) * np.float32(0.9)
    return horizontal, vertical


def padded(pixels):
    return -(-pixels // 256) * 256


def match_kernel(info, row_v, col_u, *refs, halo, slots, pixels):
    if halo:
        features, prev, after, out, src_buf, tgt_buf, sems = refs
    else:
        features, out, src_buf, tgt_buf, sems = refs
    count = info[0]
    wide = src_buf.shape[1]
    tile = wide // P_TILES
    for buf in range(2):
        src_buf[buf, pixels:, :] = jnp.zeros((wide - pixels, src_buf.shape[2]), jnp.bfloat16)

    def src_copy(i, buf):
        return pltpu.make_async_copy(
            features.at[info[1 + slots + i]], src_buf.at[buf, pl.ds(0, pixels)], sems.at[0, buf]
        )

    def tgt_copy(ref, index, buf):
        return pltpu.make_async_copy(ref.at[index], tgt_buf.at[buf], sems.at[1, buf])

    def start(i, buf):
        src_copy(i, buf).start()
        which = info[1 + 2 * slots + i]
        if halo:

            @pl.when(which == 0)
            def _():
                tgt_copy(prev, 0, buf).start()

            @pl.when(which != 0)
            def _():
                tgt_copy(after, 0, buf).start()
        else:
            tgt_copy(features, which, buf).start()

    @pl.when(count > 0)
    def _():
        start(0, 0)

    def one_slot(i, carry):
        buf = lax.rem(i, 2)

        @pl.when(i + 1 < count)
        def _():
            start(i + 1, 1 - buf)

        src_copy(i, buf).wait()
        tgt_copy(features, 0, buf).wait()
        slot = info[1 + i]

        def one_tile(step, carry):
            begin = pl.multiple_of(step * tile, 128)
            source = src_buf[buf, pl.ds(begin, tile), :] * jnp.bfloat16(0.0625)
            scores = lax.dot_general(
                tgt_buf[buf],
                source,
                (((1,), (1,)), ((), ())),
                preferred_element_type=jnp.float32,
            )
            squared = scores * scores
            weights = squared * squared * squared
            by_col = jnp.zeros((IMG_W, tile), jnp.float32)
            sum_y = jnp.zeros((8, tile), jnp.float32)
            for row in range(IMG_H):
                part = weights[row * IMG_W : (row + 1) * IMG_W]
                by_col = by_col + part
                row_sum = part[0:8]
                for j in range(8, IMG_W, 8):
                    row_sum = row_sum + part[j : j + 8]
                sum_y = sum_y + row_sum * row_v[row]
            where = (pl.ds(slot, 1), pl.ds(begin, tile))
            out[(0,) + where] = jnp.sum(by_col * col_u[:, 0:1], 0, keepdims=True)
            out[(1,) + where] = jnp.sum(sum_y, 0, keepdims=True)
            out[(2,) + where] = jnp.sum(by_col, 0, keepdims=True)
            return carry

        return lax.fori_loop(0, P_TILES, one_tile, carry)

    lax.fori_loop(0, count, one_slot, 0)


def match(info, row_v, col_u, features, halo, slots):
    pixels, channels = features.shape[1:]
    wide = padded(pixels)
    smem = pl.BlockSpec(memory_space=pltpu.SMEM)
    vmem = pl.BlockSpec(memory_space=pltpu.VMEM)
    hbm = pl.BlockSpec(memory_space=pl.ANY)
    return pl.pallas_call(
        functools.partial(match_kernel, halo=bool(halo), slots=slots, pixels=pixels),
        out_shape=jax.ShapeDtypeStruct((3, ROWS, wide), jnp.float32),
        in_specs=[smem, smem, vmem] + [hbm] * (1 + len(halo)),
        out_specs=vmem,
        scratch_shapes=[
            pltpu.VMEM((2, wide, channels), jnp.bfloat16),
            pltpu.VMEM((2, pixels, channels), jnp.bfloat16),
            pltpu.SemaphoreType.DMA((2, 2)),
        ],
        compiler_params=pltpu.CompilerParams(vmem_limit_bytes=60 * 2**20),
        cost_estimate=pl.CostEstimate(
            flops=4 * pixels * pixels * channels * 2,
            bytes_accessed=8 * pixels * channels,
            transcendentals=0,
        ),
    )(info, row_v, col_u, features, *halo)


def geometry(frames, params, grid, inv_depth, depth, slots):
    depth[...] = jnp.zeros_like(depth)
    pixels = inv_depth.shape[1]
    for slot in range(slots):
        depth[slot : slot + 1, :pixels] = inv_depth[pl.ds(frames[slot], 1), :]
    d = depth[...]
    t_x, t_y, t_z, valid = (params[:, i : i + 1] for i in range(4))
    mask = valid * grid[2:3, :]
    den = 1.0 + d * t_z
    x = (grid[0:1, :] + d * t_x) / den
    y = (grid[1:2, :] + d * t_y) / den
    g_x = (t_x - x * t_z) / den * mask
    g_y = (t_y - y * t_z) / den * mask
    e = d / den * mask
    zero = jnp.zeros_like(e)
    jac_x = [e, zero, -e * x, -x * y * mask, (1.0 + x * x) * mask, -y * mask]
    jac_y = [zero, e, -e * y, -(1.0 + y * y) * mask, x * y * mask, x * mask]
    coupling = [a * g_x + b * g_y for a, b in zip(jac_x, jac_y)]
    hess = DAMPING + over_source(params, g_x * g_x + g_y * g_y, slots)
    return x, y, mask, g_x, g_y, jac_x, jac_y, coupling, hess


def over_source(params, value, slots):
    return sum(params[:, 8 + s : 9 + s] * value[s : s + 1, :] for s in range(slots))


def band_kernel(frames, params, same, grid, inv_depth, out, depth, *, slots, pixels):
    _, _, _, _, _, jac_x, jac_y, coupling, hess = geometry(
        frames, params, grid, inv_depth, depth, slots
    )

    def gram(a, b):
        return lax.dot_general(
            a, b, (((1,), (1,)), ((), ())), precision=HIGHEST_PREC, preferred_element_type=jnp.float32
        )

    inverse = 1.0 / hess
    jac_x = jnp.concatenate(jac_x, 0)
    jac_y = jnp.concatenate(jac_y, 0)
    scaled = jnp.concatenate([c * inverse for c in coupling], 0)
    coupling = jnp.concatenate(coupling, 0)
    schur = gram(scaled, coupling)
    normal = gram(jac_x, jac_x) + gram(jac_y, jac_y)
    row = lax.broadcasted_iota(jnp.int32, normal.shape, 0)
    col = lax.broadcasted_iota(jnp.int32, normal.shape, 1)
    normal = jnp.where(row % ROWS == col % ROWS, normal, 0.0)
    out[...] = (normal - same[...] * schur) / pixels


def rhs_kernel(frames, params, grid, inv_depth, *refs, slots, pixels):
    *sums, out, depth = refs
    x, y, mask, g_x, g_y, jac_x, jac_y, coupling, hess = geometry(
        frames, params, grid, inv_depth, depth, slots
    )
    kind = params[:, 4:5]
    valid = params[:, 3:4] > 0

    def chosen(index):
        value = sums[-1][index]
        for i in range(len(sums) - 1):
            value = jnp.where(kind == float(i), sums[i][index], value)
        return jnp.where(valid, value, 0.0)

    total = chosen(2) + FLOOR / 8
    r_x = (chosen(0) / total - x) * mask
    r_y = (chosen(1) / total - y) * mask
    pull = over_source(params, g_x * r_x + g_y * r_y, slots) / hess
    lane = lax.broadcasted_iota(jnp.int32, out.shape, 1)
    result = jnp.zeros(out.shape, jnp.float32)
    for i in range(6):
        value = jnp.sum(jac_x[i] * r_x + jac_y[i] * r_y - coupling[i] * pull, 1, keepdims=True)
        result = jnp.where(lane == i, value, result)
    out[...] = result / pixels


def small_call(kernel, shape, operands, slots, pixels):
    smem = pl.BlockSpec(memory_space=pltpu.SMEM)
    vmem = pl.BlockSpec(memory_space=pltpu.VMEM)
    return pl.pallas_call(
        functools.partial(kernel, slots=slots, pixels=pixels),
        out_shape=jax.ShapeDtypeStruct(shape, jnp.float32),
        in_specs=[smem] + [vmem] * (len(operands) - 1),
        out_specs=vmem,
        scratch_shapes=[pltpu.VMEM((ROWS, padded(pixels)), jnp.float32)],
        compiler_params=pltpu.CompilerParams(vmem_limit_bytes=40 * 2**20),
    )(*operands)


def rim_sums(window, frames_dev):
    from_next = from_behind(window[:, :SPAN], -1)
    from_prev = from_behind(window[:, SPAN + frames_dev :], 1)
    own = window[:, SPAN : SPAN + frames_dev]
    zeros = jnp.zeros((window.shape[0], frames_dev - SPAN), jnp.float32)
    return own + jnp.concatenate([from_prev, zeros], 1) + jnp.concatenate([zeros, from_next], 1)


def on_device(features, inv_depth, positions, edge_list, edge_counts):
    frames_dev, pixels, _ = features.shape
    slots = edge_list.shape[0]
    total_frames = positions.shape[1]
    first_frame = lax.axis_index(AXES) * frames_dev

    slot_ids = jnp.arange(slots, dtype=jnp.int32)
    valid = (slot_ids < edge_counts[0]) & (edge_list[:, 0] >= 0)
    source = jnp.clip(edge_list[:, 0], 0, total_frames - 1)
    target = jnp.clip(edge_list[:, 1], 0, total_frames - 1)
    src = jnp.clip(source - first_frame, 0, frames_dev - 1)
    tgt = target - first_frame
    before = -tgt
    behind = tgt - frames_dev + 1

    def first_of(distance):
        needs = valid & (distance >= 1) & (distance <= SPAN)
        pick = jnp.min(jnp.where(needs, slot_ids * (SPAN + 1) + distance, slots * (SPAN + 1) + 1))
        return jnp.where(pick < slots * (SPAN + 1), pick % (SPAN + 1), 1).astype(jnp.int32)

    want_prev, want_next = first_of(before), first_of(behind)
    asked_by_prev = jnp.clip(from_behind(want_next[None], 1)[0], 1, SPAN)
    asked_by_next = jnp.clip(from_behind(want_prev[None], -1)[0], 1, SPAN)

    def frame(index):
        return lax.dynamic_slice_in_dim(features, index, 1, axis=0)

    near_after = from_behind(frame(asked_by_prev - 1), -1)
    near_prev = from_behind(frame(frames_dev - asked_by_next), 1)
    rest_head = frame(SPAN - asked_by_prev)
    rest_tail = frame(frames_dev - (SPAN + 1) + asked_by_next)
    rest_head, rest_tail, near_prev, near_after = lax.optimization_barrier(
        (rest_head, rest_tail, near_prev, near_after)
    )
    far_after = from_behind(rest_head, -1)
    far_prev = from_behind(rest_tail, 1)

    is_before, is_behind = before >= 1, behind >= 1
    asked = (is_before & (before == want_prev)) | (is_behind & (behind == want_next))
    kind = jnp.where(is_before | is_behind, jnp.where(asked, 1, 2), 0)
    halo_id = is_behind.astype(jnp.int32)

    def info_of(which):
        member = valid & (kind == which)
        earlier = member[None, :] & (slot_ids[None, :] < slot_ids[:, None])
        rank = jnp.sum(earlier.astype(jnp.int32), 1)
        place = (member[None, :] & (rank[None, :] == slot_ids[:, None])).astype(jnp.int32)
        index = jnp.clip(tgt, 0, frames_dev - 1) if which == 0 else halo_id
        count = jnp.sum(member.astype(jnp.int32))
        lists = [jnp.sum(place * v[None, :], 1) for v in (slot_ids, src, index)]
        return jnp.concatenate([count[None]] + lists).astype(jnp.int32)

    horizontal, vertical = pixel_grid()
    rounded_u = jnp.asarray(horizontal[:IMG_W]).astype(jnp.bfloat16).astype(jnp.float32)
    rounded_v = jnp.asarray(vertical[::IMG_W]).astype(jnp.bfloat16).astype(jnp.float32)
    col_u = jnp.broadcast_to(rounded_u[:, None], (IMG_W, 128))
    table = np.zeros((8, padded(pixels)), np.float32)
    table[0, :pixels] = horizontal
    table[1, :pixels] = vertical
    table[2, :pixels] = 1.0
    grid = jnp.asarray(table)

    sums = [
        match(info_of(0), rounded_v, col_u, features, (), slots),
        match(info_of(1), rounded_v, col_u, features, (near_prev, near_after), slots),
        match(info_of(2), rounded_v, col_u, features, (far_prev, far_after), slots),
    ]

    motion = (positions[:, target] - positions[:, source]).T
    same = (src[:, None] == src[None, :]) & valid[:, None] & valid[None, :]
    same = jnp.pad(same.astype(jnp.float32), ((0, ROWS - slots), (0, ROWS - slots)))
    columns = jnp.concatenate(
        [motion, valid.astype(jnp.float32)[:, None], kind.astype(jnp.float32)[:, None]], 1
    )
    columns = jnp.pad(columns, ((0, ROWS - slots), (0, 3)))
    params = jnp.pad(jnp.concatenate([columns, same], 1), ((0, 0), (0, 112)))

    blocks = small_call(
        band_kernel,
        (6 * ROWS, 6 * ROWS),
        (src, params, jnp.tile(same, (6, 6)), grid, inv_depth),
        slots,
        pixels,
    )
    window = frames_dev + 2 * SPAN
    pose = jnp.arange(window + OFFSETS - 1, dtype=jnp.int32)[:, None] - SPAN
    ends = (pose == tgt[None, :]).astype(jnp.float32) - (pose == src[None, :]).astype(jnp.float32)
    ends = ends * valid.astype(jnp.float32)[None, :]
    shifted = jnp.stack([ends[k : k + window] for k in range(OFFSETS)])
    pairs = ends[None, :window, :, None] * shifted[:, :, None, :]
    blocks = blocks.reshape(6, ROWS, 6, ROWS)[:, :slots, :, :slots]
    band = jnp.einsum("kmst,isjt->kijm", pairs, blocks, precision=HIGHEST_PREC)
    band = rim_sums(band.reshape(OFFSETS * 36, window), frames_dev)

    sides = small_call(rhs_kernel, (ROWS, 128), (src, params, grid, inv_depth, *sums), slots, pixels)
    rhs = jnp.sum(sides[:slots, :6, None] * ends[:window].T[:, None, :], 0)
    rhs = rim_sums(rhs, frames_dev)
    return band.reshape(OFFSETS, 36, frames_dev), rhs


def solution(mesh):
    in_specs = (P(AXES, None, None), P(AXES, None), P(), P(AXES, None), P(AXES))
    out_specs = (P(None, None, AXES), P(None, AXES))
    return jax.shard_map(
        on_device, mesh=mesh, in_specs=in_specs, out_specs=out_specs, check_vma=False
    )
```

```python
import functools

import jax
import jax.numpy as jnp
import numpy as np
from jax import lax
from jax.experimental import pallas as pl
from jax.experimental.pallas import tpu as pltpu
from jax.sharding import PartitionSpec as P

IMG_H = 60
IMG_W = 80
SPAN = 2
DAMPING = 0.02
FLOOR = 0.001
HIGHEST_PREC = lax.Precision.HIGHEST
AXES = ("grp", "dev")
ROWS = 8
P_TILES = 2
OFFSETS = 2 * SPAN + 1


def from_behind(value, steps):
    count = lax.axis_size(AXES)
    first, last = (max(0, -steps), min(count, count - steps))
    return lax.ppermute(value, AXES, [(source, source + steps) for source in range(first, last)])


def pixel_grid():
    index = np.arange(IMG_H * IMG_W)
    row = (index // IMG_W).astype(np.float32)
    col = (index % IMG_W).astype(np.float32)
    half = np.float32(0.5)
    horizontal = ((col + half) / np.float32(IMG_W) - half) * np.float32(1.2)
    vertical = ((row + half) / np.float32(IMG_H) - half) * np.float32(0.9)
    return horizontal, vertical


def padded(pixels):
    return -(-pixels // 256) * 256


def match_kernel(info, row_v, col_u, *refs, halo, slots, pixels):
    if halo:
        features, prev, after, out, src_buf, tgt_buf, sems = refs
    else:
        features, out, src_buf, tgt_buf, sems = refs
    count = info[0]
    wide = src_buf.shape[1]
    tile = wide // P_TILES
    for buf in range(2):
        src_buf[buf, pixels:, :] = jnp.zeros((wide - pixels, src_buf.shape[2]), jnp.bfloat16)

    def src_copy(i, buf):
        return pltpu.make_async_copy(
            features.at[info[1 + slots + i]], src_buf.at[buf, pl.ds(0, pixels)], sems.at[0, buf]
        )

    def tgt_copy(ref, index, buf):
        return pltpu.make_async_copy(ref.at[index], tgt_buf.at[buf], sems.at[1, buf])

    def start(i, buf):
        src_copy(i, buf).start()
        which = info[1 + 2 * slots + i]
        if halo:

            @pl.when(which == 0)
            def _():
                tgt_copy(prev, 0, buf).start()

            @pl.when(which != 0)
            def _():
                tgt_copy(after, 0, buf).start()
        else:
            tgt_copy(features, which, buf).start()

    @pl.when(count > 0)
    def _():
        start(0, 0)

    def one_slot(i, carry):
        buf = lax.rem(i, 2)

        @pl.when(i + 1 < count)
        def _():
            start(i + 1, 1 - buf)

        src_copy(i, buf).wait()
        tgt_copy(features, 0, buf).wait()
        slot = info[1 + i]

        def one_tile(step, carry):
            begin = pl.multiple_of(step * tile, 128)
            source = src_buf[buf, pl.ds(begin, tile), :] * jnp.bfloat16(0.0625)
            scores = lax.dot_general(
                tgt_buf[buf],
                source,
                (((1,), (1,)), ((), ())),
                preferred_element_type=jnp.float32,
            )
            squared = scores * scores
            weights = squared * squared * squared
            by_col = jnp.zeros((IMG_W, tile), jnp.float32)
            sum_y = jnp.zeros((8, tile), jnp.float32)
            for row in range(IMG_H):
                part = weights[row * IMG_W : (row + 1) * IMG_W]
                by_col = by_col + part
                row_sum = part[0:8]
                for j in range(8, IMG_W, 8):
                    row_sum = row_sum + part[j : j + 8]
                sum_y = sum_y + row_sum * row_v[row]
            where = (pl.ds(slot, 1), pl.ds(begin, tile))
            out[(0,) + where] = jnp.sum(by_col * col_u[:, 0:1], 0, keepdims=True)
            out[(1,) + where] = jnp.sum(sum_y, 0, keepdims=True)
            out[(2,) + where] = jnp.sum(by_col, 0, keepdims=True)
            return carry

        return lax.fori_loop(0, P_TILES, one_tile, carry)

    lax.fori_loop(0, count, one_slot, 0)


def match(info, row_v, col_u, features, halo, slots):
    pixels, channels = features.shape[1:]
    wide = padded(pixels)
    smem = pl.BlockSpec(memory_space=pltpu.SMEM)
    vmem = pl.BlockSpec(memory_space=pltpu.VMEM)
    hbm = pl.BlockSpec(memory_space=pl.ANY)
    return pl.pallas_call(
        functools.partial(match_kernel, halo=bool(halo), slots=slots, pixels=pixels),
        out_shape=jax.ShapeDtypeStruct((3, ROWS, wide), jnp.float32),
        in_specs=[smem, smem, vmem] + [hbm] * (1 + len(halo)),
        out_specs=vmem,
        scratch_shapes=[
            pltpu.VMEM((2, wide, channels), jnp.bfloat16),
            pltpu.VMEM((2, pixels, channels), jnp.bfloat16),
            pltpu.SemaphoreType.DMA((2, 2)),
        ],
        compiler_params=pltpu.CompilerParams(vmem_limit_bytes=60 * 2**20),
        cost_estimate=pl.CostEstimate(
            flops=4 * pixels * pixels * channels * 2,
            bytes_accessed=8 * pixels * channels,
            transcendentals=0,
        ),
    )(info, row_v, col_u, features, *halo)


def geometry(frames, params, grid, inv_depth, depth, slots):
    depth[...] = jnp.zeros_like(depth)
    pixels = inv_depth.shape[1]
    for slot in range(slots):
        depth[slot : slot + 1, :pixels] = inv_depth[pl.ds(frames[slot], 1), :]
    d = depth[...]
    t_x, t_y, t_z, valid = (params[:, i : i + 1] for i in range(4))
    mask = valid * grid[2:3, :]
    den = 1.0 + d * t_z
    x = (grid[0:1, :] + d * t_x) / den
    y = (grid[1:2, :] + d * t_y) / den
    g_x = (t_x - x * t_z) / den * mask
    g_y = (t_y - y * t_z) / den * mask
    e = d / den * mask
    zero = jnp.zeros_like(e)
    jac_x = [e, zero, -e * x, -x * y * mask, (1.0 + x * x) * mask, -y * mask]
    jac_y = [zero, e, -e * y, -(1.0 + y * y) * mask, x * y * mask, x * mask]
    coupling = [a * g_x + b * g_y for a, b in zip(jac_x, jac_y)]
    hess = DAMPING + over_source(params, g_x * g_x + g_y * g_y, slots)
    return x, y, mask, g_x, g_y, jac_x, jac_y, coupling, hess


def over_source(params, value, slots):
    return sum(params[:, 8 + s : 9 + s] * value[s : s + 1, :] for s in range(slots))


def band_kernel(frames, params, same, grid, inv_depth, out, depth, *, slots, pixels):
    _, _, _, _, _, jac_x, jac_y, coupling, hess = geometry(
        frames, params, grid, inv_depth, depth, slots
    )

    def gram(a, b):
        return lax.dot_general(
            a, b, (((1,), (1,)), ((), ())), precision=HIGHEST_PREC, preferred_element_type=jnp.float32
        )

    inverse = 1.0 / hess
    jac_x = jnp.concatenate(jac_x, 0)
    jac_y = jnp.concatenate(jac_y, 0)
    scaled = jnp.concatenate([c * inverse for c in coupling], 0)
    coupling = jnp.concatenate(coupling, 0)
    schur = gram(scaled, coupling)
    normal = gram(jac_x, jac_x) + gram(jac_y, jac_y)
    row = lax.broadcasted_iota(jnp.int32, normal.shape, 0)
    col = lax.broadcasted_iota(jnp.int32, normal.shape, 1)
    normal = jnp.where(row % ROWS == col % ROWS, normal, 0.0)
    out[...] = (normal - same[...] * schur) / pixels


def rhs_kernel(frames, params, grid, inv_depth, *refs, slots, pixels):
    *sums, out, depth = refs
    x, y, mask, g_x, g_y, jac_x, jac_y, coupling, hess = geometry(
        frames, params, grid, inv_depth, depth, slots
    )
    kind = params[:, 4:5]
    valid = params[:, 3:4] > 0

    def chosen(index):
        value = sums[-1][index]
        for i in range(len(sums) - 1):
            value = jnp.where(kind == float(i), sums[i][index], value)
        return jnp.where(valid, value, 0.0)

    total = chosen(2) + FLOOR / 8
    r_x = (chosen(0) / total - x) * mask
    r_y = (chosen(1) / total - y) * mask
    pull = over_source(params, g_x * r_x + g_y * r_y, slots) / hess
    lane = lax.broadcasted_iota(jnp.int32, out.shape, 1)
    result = jnp.zeros(out.shape, jnp.float32)
    for i in range(6):
        value = jnp.sum(jac_x[i] * r_x + jac_y[i] * r_y - coupling[i] * pull, 1, keepdims=True)
        result = jnp.where(lane == i, value, result)
    out[...] = result / pixels


def small_call(kernel, shape, operands, slots, pixels):
    smem = pl.BlockSpec(memory_space=pltpu.SMEM)
    vmem = pl.BlockSpec(memory_space=pltpu.VMEM)
    return pl.pallas_call(
        functools.partial(kernel, slots=slots, pixels=pixels),
        out_shape=jax.ShapeDtypeStruct(shape, jnp.float32),
        in_specs=[smem] + [vmem] * (len(operands) - 1),
        out_specs=vmem,
        scratch_shapes=[pltpu.VMEM((ROWS, padded(pixels)), jnp.float32)],
        compiler_params=pltpu.CompilerParams(vmem_limit_bytes=40 * 2**20),
    )(*operands)


def rim_sums(window, frames_dev):
    from_next = from_behind(window[:, :SPAN], -1)
    from_prev = from_behind(window[:, SPAN + frames_dev :], 1)
    own = window[:, SPAN : SPAN + frames_dev]
    zeros = jnp.zeros((window.shape[0], frames_dev - SPAN), jnp.float32)
    return own + jnp.concatenate([from_prev, zeros], 1) + jnp.concatenate([zeros, from_next], 1)


def on_device(features, inv_depth, positions, edge_list, edge_counts):
    frames_dev, pixels, _ = features.shape
    slots = edge_list.shape[0]
    total_frames = positions.shape[1]
    first_frame = lax.axis_index(AXES) * frames_dev

    slot_ids = jnp.arange(slots, dtype=jnp.int32)
    valid = (slot_ids < edge_counts[0]) & (edge_list[:, 0] >= 0)
    source = jnp.clip(edge_list[:, 0], 0, total_frames - 1)
    target = jnp.clip(edge_list[:, 1], 0, total_frames - 1)
    src = jnp.clip(source - first_frame, 0, frames_dev - 1)
    tgt = target - first_frame
    before = -tgt
    behind = tgt - frames_dev + 1

    def first_of(distance):
        needs = valid & (distance >= 1) & (distance <= SPAN)
        pick = jnp.min(jnp.where(needs, slot_ids * (SPAN + 1) + distance, slots * (SPAN + 1) + 1))
        return jnp.where(pick < slots * (SPAN + 1), pick % (SPAN + 1), 1).astype(jnp.int32)

    want_prev, want_next = first_of(before), first_of(behind)
    asked_by_prev = jnp.clip(from_behind(want_next[None], 1)[0], 1, SPAN)
    asked_by_next = jnp.clip(from_behind(want_prev[None], -1)[0], 1, SPAN)

    def frame(index):
        return lax.dynamic_slice_in_dim(features, index, 1, axis=0)

    head, tail = frame(asked_by_prev - 1), frame(frames_dev - asked_by_next)

    is_before, is_behind = before >= 1, behind >= 1
    asked = (is_before & (before == want_prev)) | (is_behind & (behind == want_next))
    kind = jnp.where(is_before | is_behind, jnp.where(asked, 1, 2), 0)
    halo_id = is_behind.astype(jnp.int32)

    def info_of(which):
        member = valid & (kind == which)
        earlier = member[None, :] & (slot_ids[None, :] < slot_ids[:, None])
        rank = jnp.sum(earlier.astype(jnp.int32), 1)
        place = (member[None, :] & (rank[None, :] == slot_ids[:, None])).astype(jnp.int32)
        index = jnp.clip(tgt, 0, frames_dev - 1) if which == 0 else halo_id
        count = jnp.sum(member.astype(jnp.int32))
        lists = [jnp.sum(place * v[None, :], 1) for v in (slot_ids, src, index)]
        return jnp.concatenate([count[None]] + lists).astype(jnp.int32)

    horizontal, vertical = pixel_grid()
    rounded_u = jnp.asarray(horizontal[:IMG_W]).astype(jnp.bfloat16).astype(jnp.float32)
    rounded_v = jnp.asarray(vertical[::IMG_W]).astype(jnp.bfloat16).astype(jnp.float32)
    col_u = jnp.broadcast_to(rounded_u[:, None], (IMG_W, 128))
    table = np.zeros((8, padded(pixels)), np.float32)
    table[0, :pixels] = horizontal
    table[1, :pixels] = vertical
    table[2, :pixels] = 1.0
    grid = jnp.asarray(table)

    need_far = jnp.any(valid & (kind == 2)).astype(jnp.int32)
    any_far = lax.pmax(need_far, AXES) > 0
    info = [info_of(which) for which in range(3)]
    (head, tail, first_info, positions, src, tgt, valid, kind, asked_by_prev, asked_by_next) = (
        lax.optimization_barrier(
            (head, tail, info[0], positions, src, tgt, valid, kind, asked_by_prev, asked_by_next)
        )
    )
    near_after = from_behind(head, -1)
    near_prev = from_behind(tail, 1)
    local_sums = match(first_info, rounded_v, col_u, features, (), slots)
    halo_sums = match(info[1], rounded_v, col_u, features, (near_prev, near_after), slots)

    source, target = src + first_frame, jnp.clip(tgt + first_frame, 0, total_frames - 1)

    def with_far(near):
        far_after = from_behind(frame(SPAN - asked_by_prev), -1)
        far_prev = from_behind(frame(frames_dev - (SPAN + 1) + asked_by_next), 1)
        far = match(info[2], rounded_v, col_u, features, (far_prev, far_after), slots)
        is_far = jnp.pad(kind == 2, (0, ROWS - slots))
        return jnp.where(is_far[None, :, None], far, near)

    sums = [local_sums, lax.cond(any_far, with_far, lambda near: near, halo_sums)]

    motion = (positions[:, target] - positions[:, source]).T
    same = (src[:, None] == src[None, :]) & valid[:, None] & valid[None, :]
    same = jnp.pad(same.astype(jnp.float32), ((0, ROWS - slots), (0, ROWS - slots)))
    columns = jnp.concatenate(
        [motion, valid.astype(jnp.float32)[:, None], kind.astype(jnp.float32)[:, None]], 1
    )
    columns = jnp.pad(columns, ((0, ROWS - slots), (0, 3)))
    params = jnp.pad(jnp.concatenate([columns, same], 1), ((0, 0), (0, 112)))

    blocks = small_call(
        band_kernel,
        (6 * ROWS, 6 * ROWS),
        (src, params, jnp.tile(same, (6, 6)), grid, inv_depth),
        slots,
        pixels,
    )
    window = frames_dev + 2 * SPAN
    pose = jnp.arange(window + OFFSETS - 1, dtype=jnp.int32)[:, None] - SPAN
    ends = (pose == tgt[None, :]).astype(jnp.float32) - (pose == src[None, :]).astype(jnp.float32)
    ends = ends * valid.astype(jnp.float32)[None, :]
    shifted = jnp.stack([ends[k : k + window] for k in range(OFFSETS)])
    pairs = ends[None, :window, :, None] * shifted[:, :, None, :]
    blocks = blocks.reshape(6, ROWS, 6, ROWS)[:, :slots, :, :slots]
    band = jnp.einsum("kmst,isjt->kijm", pairs, blocks, precision=HIGHEST_PREC)
    band = band.reshape(OFFSETS * 36, window)

    sides = small_call(rhs_kernel, (ROWS, 128), (src, params, grid, inv_depth, *sums), slots, pixels)
    rhs = jnp.sum(sides[:slots, :6, None] * ends[:window].T[:, None, :], 0)
    both = rim_sums(jnp.concatenate([band, rhs], 0), frames_dev)
    return both[: OFFSETS * 36].reshape(OFFSETS, 36, frames_dev), both[OFFSETS * 36 :]


def solution(mesh):
    in_specs = (P(AXES, None, None), P(AXES, None), P(), P(AXES, None), P(AXES))
    out_specs = (P(None, None, AXES), P(None, AXES))
    return jax.shard_map(
        on_device, mesh=mesh, in_specs=in_specs, out_specs=out_specs, check_vma=False
    )
```
